32 devices in a mesh: gx: 4 (over x, core), ev: 8 (over z, y).
Axes of the slice: x: 2, y: 2, z: 4, core: 2. Of those that a mesh axis runs over, the one named last changes fastest.
Arguments:
- partial_kernels: bfloat16 [8, 2048, 2, 8, 2048], P('ev', 'gx'), may hold values from -8 to 8
- illumination: float32 [2048, 8, 2048], P('gx', None, 'ev'), may hold values from 0.3 to 3
- classes_x: int32 [8, 2048], P(None, 'ev'), may hold values from 0 to 2
- classes_y: int32 [2048, 8], P('gx'), may hold values from 0 to 2
- widths_x: float32 [3], replicated, may hold values from 0.5 to 1
- widths_y: float32 [3], replicated, may hold values from 0.5 to 1
Outputs:
- conditioned: bfloat16 [2048, 2, 8, 2048], P('gx', None, None, 'ev')
The draws below stay inside these ranges and needn't reach their ends.
All inputs are finite; a program needn't handle non-finite values.
Results may differ from the reference program's by a relative error of at most 0.0035.
Values may be sent and summed in bfloat16 or wider, within the bound.
No kernel may reach another device: no remote copies, remote signals or barrier semaphores. Data moves between devices by JAX's collectives and lax.ppermute only.
A program may use at most 192 MiB of HBM per device.

```python
import math
import jax
import jax.numpy as jnp
from jax import lax

NX = 2048
NY = 2048
KERNELS = 2
NZ = 8
CLASSES = 3
BAND = 128
GROUPS = 8


def draw_partial_kernels(key, part):
    streams = jax.random.split(key, 6)
    extent = (GROUPS, NX, KERNELS, NZ, NY)
    per_map = (GROUPS, 1, KERNELS, NZ, 1)
    noise_part = jnp.clip(jax.random.normal(streams[0], extent, jnp.float32), -5.0, 5.0)
    wave_x = jax.random.randint(streams[1], per_map, 1, 4).astype(jnp.float32)
    wave_y = jax.random.randint(streams[2], per_map, 1, 4).astype(jnp.float32)
    phase_x = jax.random.uniform(streams[3], per_map, jnp.float32, 0.0, 2.0 * math.pi)
    phase_y = jax.random.uniform(streams[4], per_map, jnp.float32, 0.0, 2.0 * math.pi)
    height = jax.random.uniform(streams[5], per_map, jnp.float32, 0.5, 1.5)
    grid_x = (jnp.arange(NX, dtype=jnp.float32) / NX).reshape(1, NX, 1, 1, 1)
    grid_y = (jnp.arange(NY, dtype=jnp.float32) / NY).reshape(1, 1, 1, 1, NY)
    smooth = height * jnp.cos(2.0 * math.pi * wave_x * grid_x + phase_x) * jnp.cos(2.0 * math.pi * wave_y * grid_y + phase_y)
    return (noise_part + 1.5 * smooth).astype(jnp.bfloat16)


def touch_ends(values, own_key, smallest, top_value):
    shape = values.shape
    index_at = [jax.random.randint(jax.random.fold_in(own_key, axis), (), 0, shape[axis]) for axis in range(len(shape))]
    values = values.at[tuple(index_at)].set(smallest)
    longest = shape.index(max(shape))
    index_at[longest] = (index_at[longest] + 1) % shape[longest]
    return values.at[tuple(index_at)].set(top_value)


def block_levels(stream_key, shape, cuts, least, top_value):
    gain, own = 1.0, jax.random.fold_in(stream_key, 6)
    for position, shards_of in cuts:
        heights = jnp.exp(jax.random.uniform(jax.random.fold_in(own, position), (shards_of,), jnp.float32, least / len(cuts), top_value / len(cuts)))
        gain = gain * jnp.repeat(heights, shape[position] // shards_of).reshape([-1 if axis == position else 1 for axis in range(len(shape))])
    return gain


def setup_inputs(seed: int = 0) -> dict:
    key_list = jax.random.split(jax.random.key(seed), 7)
    return {
        "partial_kernels": draw_partial_kernels(jax.random.fold_in(key_list[6], 71), 0),
        "illumination": jnp.clip(jnp.exp(math.log(3.0) - 2.3025851 * jax.random.uniform(key_list[1], (NX, NZ, NY), jnp.float32) ** block_levels(key_list[1], (NX, NZ, NY), ((0, 4), (2, 8)), -0.2, 0.2)), 0.3, 3.0),
        "classes_x": touch_ends(jax.random.randint(key_list[2], (NZ, NY), 0, CLASSES), jax.random.fold_in(key_list[2], 1), 0, CLASSES - 1).astype(jnp.int32),
        "classes_y": touch_ends(jax.random.randint(key_list[3], (NX, NZ), 0, CLASSES), jax.random.fold_in(key_list[3], 1), 0, CLASSES - 1).astype(jnp.int32),
        "widths_x": jnp.clip(jnp.exp(jax.random.uniform(key_list[4], (CLASSES,), jnp.float32, math.log(0.5), math.log(1.0))), 0.5, 1.0),
        "widths_y": jnp.clip(jnp.exp(jax.random.uniform(key_list[5], (CLASSES,), jnp.float32, math.log(0.5), math.log(1.0))), 0.5, 1.0),
    }


blend_weight = 0.25
soft_bound = 2.0


def smoother(length, fraction):
    positions = jnp.arange(length, dtype=jnp.float32)
    offset = positions[:, None] - positions[None, :]
    distance = offset / (fraction * BAND)
    gaussian = jnp.where(jnp.abs(offset) <= BAND, jnp.exp(-0.5 * distance * distance), jnp.float32(0.0))
    gaussian = gaussian / jnp.sum(gaussian, axis=1, keepdims=True)
    return (gaussian + blend_weight * jnp.eye(length, dtype=jnp.float32)).astype(jnp.bfloat16)


def smooth_columns(columns, labels, matrices):
    summed = jnp.zeros((matrices[0].shape[0], columns.shape[1]), jnp.float32)
    for level in range(len(matrices)):
        product = jnp.dot(matrices[level], columns, preferred_element_type=jnp.float32)
        summed = summed + jnp.where(labels[None, :] == level, product, jnp.float32(0.0))
    return summed


def smooth_rows(row_block, labels, matrices):
    summed = jnp.zeros((row_block.shape[0], matrices[0].shape[0]), jnp.float32)
    for level in range(len(matrices)):
        product = lax.dot_general(row_block, matrices[level], (((1,), (1,)), ((), ())), preferred_element_type=jnp.float32)
        summed = summed + jnp.where(labels[:, None] == level, product, jnp.float32(0.0))
    return summed


def reference(partial_kernels, illumination, classes_x, classes_y, widths_x, widths_y):
    def accumulate(summed, group_term):
        return summed + group_term.astype(jnp.float32), None

    summed, unused = lax.scan(accumulate, jnp.zeros(partial_kernels.shape[1:], jnp.float32), partial_kernels)
    scaled = (summed / illumination[:, None, :, :]).astype(jnp.bfloat16)
    matrices_x = [smoother(NX, widths_x[level]) for level in range(CLASSES)]
    matrices_y = [smoother(NY, widths_y[level]) for level in range(CLASSES)]
    flattened = scaled.reshape(NX, KERNELS * NZ * NY)
    col_class = jnp.broadcast_to(classes_x[None, :, :], (KERNELS, NZ, NY)).reshape(-1)
    smoothed_x = smooth_columns(flattened, col_class, matrices_x)
    bounded = (soft_bound * jnp.tanh(smoothed_x / soft_bound)).astype(jnp.bfloat16)
    row_block = bounded.reshape(NX * KERNELS * NZ, NY)
    row_class = jnp.broadcast_to(classes_y[:, None, :], (NX, KERNELS, NZ)).reshape(-1)
    smoothed_y = smooth_rows(row_block, row_class, matrices_y)
    return smoothed_y.astype(jnp.bfloat16).reshape(NX, KERNELS, NZ, NY)
```

```python
import functools

import jax
import jax.numpy as jnp
from jax import lax
from jax.experimental import pallas as pl
from jax.experimental.pallas import tpu as pltpu
from jax.sharding import PartitionSpec as P

BAND = 128
PAIR = 2

blend_weight = 0.25
soft_bound = 2.0


def plan_chunks(kernels, half):
    lead = half // 2
    chunks = [("zy", 0, 0, lead), ("yz", 0, lead, half - lead)]
    for k in range(1, kernels):
        chunks.append(("yz", k, 0, lead))
        chunks += [("yz", k, j, 1) for j in range(lead, half)]
    return chunks


VMEM = 60 * 1024 * 1024


def params():
    return pltpu.CompilerParams(vmem_limit_bytes=VMEM)


def cost(flops, nbytes, trans=0):
    return pl.CostEstimate(flops=int(flops), bytes_accessed=int(nbytes), transcendentals=int(trans))


def split_planes(own_part, perm, kernel_id, chunks, shards, rows, after=()):
    _, slab_x, _, planes, full_y = own_part.shape
    half = planes // PAIR
    wide = full_y // shards
    span = perm.shape[0]
    sub = span // planes
    outs, specs, plan = [], [], []
    for order, _, first, slots in chunks:
        parts = ((0, half),) if order == "zy" else ((0,), (half,))
        for offsets in parts:
            count = slots * len(offsets)
            outs.append(jax.ShapeDtypeStruct((shards, count, slab_x, wide), jnp.bfloat16))
            specs.append(pl.BlockSpec((1, count, rows, wide), lambda s, i: (s, 0, i, 0)))
            plan.append([offset + first + j for offset in offsets for j in range(slots)])

    def body(part_ref, perm_ref, *refs):
        out_refs = refs[len(after) :]
        for b in range(rows // sub):
            block = part_ref[0, b * sub : (b + 1) * sub, 0].astype(jnp.float32)
            block = block.reshape(span, wide).astype(jnp.bfloat16)
            moved = jnp.dot(perm_ref[...], block, preferred_element_type=jnp.float32)
            moved = moved.astype(jnp.bfloat16).reshape(planes, sub, wide)
            for out_ref, slots_of in zip(out_refs, plan):
                for n, q in enumerate(slots_of):
                    out_ref[0, n, b * sub : (b + 1) * sub, :] = moved[q]

    return pl.pallas_call(
        body,
        grid=(shards, slab_x // rows),
        in_specs=[
            pl.BlockSpec((1, rows, 1, planes, wide), lambda s, i: (0, i, kernel_id, 0, s)),
            pl.BlockSpec(perm.shape, lambda s, i: (0, 0)),
        ]
        + [pl.BlockSpec(memory_space=pl.ANY)] * len(after),
        out_specs=specs,
        out_shape=outs,
        compiler_params=params(),
        cost_estimate=cost(0, 0),
        name="split_planes",
    )(own_part, perm, *after)


def hold(array, after):
    def body(*refs):
        del refs

    anywhere = pl.BlockSpec(memory_space=pl.ANY)
    return pl.pallas_call(
        body,
        in_specs=[anywhere] * (1 + len(after)),
        out_specs=anywhere,
        out_shape=jax.ShapeDtypeStruct(array.shape, array.dtype),
        input_output_aliases={0: 0},
        compiler_params=params(),
        cost_estimate=cost(0, 0),
        name="hold",
    )(array, *after)


def add_parts(a, b, after=()):
    shards, slots, slab_x, wide = a.shape

    def body(a_ref, b_ref, *refs):
        out_ref = refs[-1]
        out_ref[...] = (a_ref[...].astype(jnp.float32) + b_ref[...].astype(jnp.float32)).astype(jnp.bfloat16)

    spec = pl.BlockSpec((1, 1, slab_x, wide), lambda s, m: (s, m, 0, 0))
    return pl.pallas_call(
        body,
        grid=(shards, slots),
        in_specs=[spec, spec] + [pl.BlockSpec(memory_space=pl.ANY)] * len(after),
        out_specs=spec,
        out_shape=jax.ShapeDtypeStruct(a.shape, jnp.bfloat16),
        compiler_params=params(),
        cost_estimate=cost(a.size, 6 * a.size),
        name="add_parts",
    )(a, b, *after)


def scale(terms, lit, lit_pair, place, first, after=()):
    slots, slab_x, wide = terms[0].shape
    narrow = wide // PAIR
    count = len(terms)

    def body(place_ref, *refs):
        term_refs, (lit_ref, pair_ref) = refs[:count], refs[count : count + 2]
        out_ref, top_ref, bottom_ref = refs[-3:]
        left = place_ref[0] == 0
        for h in range(PAIR):
            total = term_refs[0][0, :, h * narrow : (h + 1) * narrow].astype(jnp.float32)
            for ref in term_refs[1:]:
                total = total + ref[0, :, h * narrow : (h + 1) * narrow].astype(jnp.float32)
            mine, theirs = lit_ref[0], pair_ref[0].astype(jnp.float32)
            by = jnp.where(left, mine, theirs) if h == 0 else jnp.where(left, theirs, mine)
            out_ref[0, :, h * narrow : (h + 1) * narrow] = (total / by).astype(jnp.bfloat16)
        top_ref[0] = out_ref[0, :BAND]
        bottom_ref[0] = out_ref[0, slab_x - BAND :]

    full = pl.BlockSpec((1, slab_x, wide), lambda m, place_ref: (m, 0, 0))
    edge = pl.BlockSpec((1, BAND, wide), lambda m, place_ref: (m, 0, 0))
    lit_spec = pl.BlockSpec((1, slab_x, narrow), lambda m, place_ref: (first + m, 0, 0))
    size = slots * slab_x * wide
    return pl.pallas_call(
        body,
        grid_spec=pltpu.PrefetchScalarGridSpec(
            num_scalar_prefetch=1,
            grid=(slots,),
            in_specs=[full] * count + [lit_spec, lit_spec] + [pl.BlockSpec(memory_space=pl.ANY)] * len(after),
            out_specs=[full, edge, edge],
        ),
        out_shape=[
            jax.ShapeDtypeStruct((slots, slab_x, wide), jnp.bfloat16),
            jax.ShapeDtypeStruct((slots, BAND, wide), jnp.bfloat16),
            jax.ShapeDtypeStruct((slots, BAND, wide), jnp.bfloat16),
        ],
        compiler_params=params(),
        cost_estimate=cost(size * 4, size * (2 * count + 6)),
        name="scale",
    )(place, *terms, lit, lit_pair, *after)


def band_tiles(length, widths, first, tiles, rows):
    shape = (widths.shape[0], tiles, rows, rows + 2 * BAND)
    base = first + rows * lax.broadcasted_iota(jnp.int32, shape, 1)
    row_pos = base + lax.broadcasted_iota(jnp.int32, shape, 2)
    col_pos = base - BAND + lax.broadcasted_iota(jnp.int32, shape, 3)
    offset = (row_pos - col_pos).astype(jnp.float32)
    inside = (jnp.abs(offset) <= BAND) & (col_pos >= 0) & (col_pos < length)
    distance = offset / (widths[:, None, None, None] * BAND)
    gaussian = jnp.where(inside, jnp.exp(-0.5 * distance * distance), jnp.float32(0.0))
    gaussian = gaussian / jnp.sum(gaussian, axis=3, keepdims=True)
    diagonal = jnp.where(offset == 0.0, jnp.float32(blend_weight), jnp.float32(0.0))
    return (gaussian + diagonal).astype(jnp.bfloat16)


def smooth_x(scaled, before, after, tiles_x, labels, first):
    slots, slab_x, wide = scaled.shape
    classes, tiles, rows, window = tiles_x.shape

    def body(mid_ref, before_ref, after_ref, tiles_ref, label_ref, out_ref, low_ref, high_ref, cat_ref):
        cat_ref[:BAND] = before_ref[0]
        cat_ref[BAND : BAND + slab_x] = mid_ref[0]
        cat_ref[BAND + slab_x :] = after_ref[0]
        label = label_ref[0]
        for t in range(tiles):
            columns = cat_ref[t * rows : t * rows + window]
            total = jnp.dot(tiles_ref[0, t], columns, preferred_element_type=jnp.float32)
            for level in range(1, classes):
                product = jnp.dot(tiles_ref[level, t], columns, preferred_element_type=jnp.float32)
                total = jnp.where(label == level, product, total)
            bounded = (soft_bound * jnp.tanh(total / soft_bound)).astype(jnp.bfloat16)
            out_ref[0, t * rows : (t + 1) * rows] = bounded
            low_ref[0, t * rows : (t + 1) * rows] = bounded[:, :BAND]
            high_ref[0, t * rows : (t + 1) * rows] = bounded[:, wide - BAND :]

    full = pl.BlockSpec((1, slab_x, wide), lambda m: (m, 0, 0))
    edge = pl.BlockSpec((1, BAND, wide), lambda m: (m, 0, 0))
    side = pl.BlockSpec((1, slab_x, BAND), lambda m: (m, 0, 0))
    size = slots * slab_x * wide
    return pl.pallas_call(
        body,
        grid=(slots,),
        in_specs=[
            full,
            edge,
            edge,
            pl.BlockSpec(tiles_x.shape, lambda m: (0, 0, 0, 0)),
            pl.BlockSpec((1, 1, wide), lambda m: (first + m, 0, 0)),
        ],
        out_specs=[full, side, side],
        out_shape=[
            jax.ShapeDtypeStruct((slots, slab_x, wide), jnp.bfloat16),
            jax.ShapeDtypeStruct((slots, slab_x, BAND), jnp.bfloat16),
            jax.ShapeDtypeStruct((slots, slab_x, BAND), jnp.bfloat16),
        ],
        scratch_shapes=[pltpu.VMEM((slab_x + 2 * BAND, wide), jnp.bfloat16)],
        compiler_params=params(),
        cost_estimate=cost(2 * classes * window * size, 6 * size, size),
        name="smooth_x",
    )(scaled, before, after, tiles_x, labels)


def smooth_y(bounded, before, after, tiles_y, labels, place, first):
    slots, slab_x, wide = bounded.shape
    classes, tiles, window, narrow = tiles_y.shape

    def body(place_ref, mid_ref, before_ref, after_ref, tiles_ref, label_ref, keep_ref, send_ref, cat_ref):
        cat_ref[:, :BAND] = before_ref[0]
        cat_ref[:, BAND : BAND + wide] = mid_ref[0]
        cat_ref[:, BAND + wide :] = after_ref[0]
        label = label_ref[0]
        left = place_ref[0] == 0
        halves = []
        for t in range(tiles):
            columns = cat_ref[:, t * narrow : t * narrow + window]
            total = jnp.dot(columns, tiles_ref[0, t], preferred_element_type=jnp.float32)
            for level in range(1, classes):
                product = jnp.dot(columns, tiles_ref[level, t], preferred_element_type=jnp.float32)
                total = jnp.where(label == level, product, total)
            halves.append(total.astype(jnp.bfloat16))
        keep_ref[0] = jnp.where(left, halves[0], halves[1])
        send_ref[0] = jnp.where(left, halves[1], halves[0])

    full = pl.BlockSpec((1, slab_x, wide), lambda m, place_ref: (m, 0, 0))
    side = pl.BlockSpec((1, slab_x, BAND), lambda m, place_ref: (m, 0, 0))
    block = pl.BlockSpec((1, slab_x, narrow), lambda m, place_ref: (m, 0, 0))
    size = slots * slab_x * wide
    out = jax.ShapeDtypeStruct((slots, slab_x, narrow), jnp.bfloat16)
    return pl.pallas_call(
        body,
        grid_spec=pltpu.PrefetchScalarGridSpec(
            num_scalar_prefetch=1,
            grid=(slots,),
            in_specs=[
                full,
                side,
                side,
                pl.BlockSpec(tiles_y.shape, lambda m, place_ref: (0, 0, 0, 0)),
                pl.BlockSpec((1, slab_x, 1), lambda m, place_ref: (first + m, 0, 0)),
            ],
            out_specs=[block, block],
            scratch_shapes=[pltpu.VMEM((slab_x, wide + 2 * BAND), jnp.bfloat16)],
        ),
        out_shape=[out, out],
        compiler_params=params(),
        cost_estimate=cost(2 * classes * window * size, 6 * size),
        name="smooth_y",
    )(place, bounded, before, after, tiles_y, labels)


def join_planes(kept, came, perm_back, slots_of, planes, rows):
    _, slab_x, narrow = kept[0].shape
    span = perm_back.shape[0]
    sub = span // planes
    half = planes // PAIR
    kernels = len(slots_of) // half
    count = len(kept)

    def body(*refs):
        kept_refs, came_refs = refs[:count], refs[count : 2 * count]
        perm_ref, out_ref, stack_ref = refs[2 * count :]
        for k in range(kernels):
            for b in range(rows // sub):
                for j in range(half):
                    c, m = slots_of[k * half + j]
                    at = slice(b * sub, (b + 1) * sub)
                    stack_ref[j * sub : (j + 1) * sub] = kept_refs[c][m, at]
                    stack_ref[(half + j) * sub : (half + j + 1) * sub] = came_refs[c][m, at]
                moved = jnp.dot(perm_ref[...], stack_ref[...], preferred_element_type=jnp.float32)
                moved = moved.reshape(sub, planes, narrow).astype(jnp.bfloat16)
                out_ref[b * sub : (b + 1) * sub, k] = moved

    specs = [pl.BlockSpec((a.shape[0], rows, narrow), lambda i: (0, i, 0)) for a in kept]
    size = slab_x * kernels * planes * narrow
    return pl.pallas_call(
        body,
        grid=(slab_x // rows,),
        in_specs=specs + specs + [pl.BlockSpec(perm_back.shape, lambda i: (0, 0))],
        out_specs=pl.BlockSpec((rows, kernels, planes, narrow), lambda i: (i, 0, 0, 0)),
        out_shape=jax.ShapeDtypeStruct((slab_x, kernels, planes, narrow), jnp.bfloat16),
        scratch_shapes=[pltpu.VMEM((span, narrow), jnp.bfloat16)],
        compiler_params=params(),
        cost_estimate=cost(2 * span * size, 4 * size),
        name="join_planes",
    )(*kept, *came, perm_back)


def per_device(partial_kernels, illumination, classes_x, classes_y, widths_x, widths_y):
    _, slab_x, kernels, planes, full_y = partial_kernels.shape
    groups = lax.axis_size("ev")
    owners = lax.axis_size("gx")
    slab_y = full_y // groups
    full_x = slab_x * owners
    shards = groups // PAIR
    half = planes // PAIR
    me = lax.axis_index("ev")
    pair = lax.rem(me, PAIR)
    line = me // PAIR
    place = pair.astype(jnp.int32).reshape(1)

    other = [(i, i ^ 1) for i in range(groups)]
    z_up = [(i, i + PAIR) for i in range(groups - PAIR)]
    z_down = [(b, a) for a, b in z_up]
    x_up = [(i, i + 1) for i in range(owners - 1)]
    x_down = [(b, a) for a, b in x_up]
    lines = [[z * PAIR + y for z in range(shards)] for y in range(PAIR)]

    def over_line(parts):
        return lax.psum_scatter(
            parts, "ev", scatter_dimension=0, axis_index_groups=lines, tiled=True
        ).reshape(parts.shape[1:])

    sub = 256 // planes
    span = sub * planes
    to_row = lax.broadcasted_iota(jnp.int32, (span, span), 0)
    from_row = lax.broadcasted_iota(jnp.int32, (span, span), 1)
    plane_of = lax.rem(to_row // sub + half * pair, planes)
    perm = (from_row == lax.rem(to_row, sub) * planes + plane_of).astype(jnp.bfloat16)
    chunks = plan_chunks(kernels, half)

    lit_planes = jnp.transpose(illumination, (1, 0, 2))
    lit = lax.dynamic_slice_in_dim(lit_planes, half * pair, half, 0)
    lit_sent = lax.dynamic_slice_in_dim(lit_planes, half * (1 - pair), half, 0).astype(jnp.bfloat16)
    lit_pair = lax.ppermute(lit_sent, "ev", other)

    split, before = {}, []
    for some in (chunks[:1], chunks[1:2], chunks[2:]):
        for k in range(kernels):
            mine = [c for c in some if c[1] == k]
            if mine:
                arrays = list(split_planes(partial_kernels, perm, k, mine, shards, slab_x, before))
                before = arrays[:1]
                for c in mine:
                    split[c] = (arrays.pop(0),) if c[0] == "zy" else (arrays.pop(0), arrays.pop(0))

    labels_mine = lax.dynamic_slice_in_dim(classes_x, half * pair, half, 0)
    labels_sent = lax.dynamic_slice_in_dim(classes_x, half * (1 - pair), half, 0)
    labels_pair = lax.ppermute(labels_sent, "ev", other)
    labels_x = jnp.where(
        pair == 0,
        jnp.concatenate([labels_mine, labels_pair], 1),
        jnp.concatenate([labels_pair, labels_mine], 1),
    ).reshape(half, 1, PAIR * slab_y)
    labels_y = lax.dynamic_slice_in_dim(classes_y.T, half * pair, half, 0).reshape(half, slab_x, 1)

    tile = min(256, slab_x)
    tiles_x = band_tiles(full_x, widths_x, lax.axis_index("gx") * slab_x, slab_x // tile, tile)
    tiles_y = jnp.swapaxes(band_tiles(full_y, widths_y, line * PAIR * slab_y, PAIR, slab_y), 2, 3)

    own, sent = split[chunks[1]]
    split[chunks[1]] = own, hold(sent, [lit_pair, split[chunks[2]][0]])

    slots_of, sums, kept, came = {}, {}, {}, {}
    for n, (order, k, first, slots) in enumerate(chunks):
        for m in range(slots):
            slots_of[k * half + first + m] = (n, m)

    def begin(n, after=()):
        order, k, first, slots = chunks[n]
        if order == "yz":
            own, sent = split[chunks[n]]
            sums[n] = [over_line(add_parts(own, lax.ppermute(sent, "ev", other), after))]
        else:
            both = over_line(split[chunks[n]][0])
            sums[n] = [both[:slots], lax.ppermute(both[slots:], "ev", other)]

    def finish(n, after=()):
        order, k, first, slots = chunks[n]
        scaled, top, bottom = scale(sums[n], lit, lit_pair, place, first, after)
        before = lax.ppermute(bottom, "gx", x_up)
        after = lax.ppermute(top, "gx", x_down)
        bounded, low, high = smooth_x(scaled, before, after, tiles_x, labels_x, first)
        before = lax.ppermute(high, "ev", z_up)
        after = lax.ppermute(low, "ev", z_down)
        kept[n], send = smooth_y(bounded, before, after, tiles_y, labels_y, place, first)
        came[n] = lax.ppermute(send, "ev", other)

    last = len(chunks)
    begin(0)
    begin(1)
    begin(2, [sums[0][1]])
    finish(1)
    begin(3, [kept[1]])
    finish(0)
    for n in range(4, last):
        begin(n, [kept[0]])
    finish(2, [kept[0], came[1]])
    for n in range(3, last):
        finish(n, [came[0]])
    order = range(last)
    return join_planes([kept[n] for n in order], [came[n] for n in order], perm.T, slots_of, planes, slab_x // 2)


def solution(mesh):
    return jax.shard_map(
        per_device,
        mesh=mesh,
        in_specs=(
            P("ev", "gx", None, None, None),
            P("gx", None, "ev"),
            P(None, "ev"),
            P("gx", None),
            P(),
            P(),
        ),
        out_specs=P("gx", None, None, "ev"),
        check_vma=False,
    )
```

```python
import functools

import jax
import jax.numpy as jnp
from jax import lax
from jax.experimental import pallas as pl
from jax.experimental.pallas import tpu as pltpu
from jax.sharding import PartitionSpec as P

BAND = 128
PAIR = 2

blend_weight = 0.25
soft_bound = 2.0


def plan_chunks(kernels, half):
    lead = half // 2
    chunks = [("zy", 0, 0, lead), ("yz", 0, lead, half - lead)]
    for k in range(1, kernels):
        chunks.append(("yz", k, 0, lead))
        chunks += [("yz", k, j, 1) for j in range(lead, half)]
    return chunks


VMEM = 60 * 1024 * 1024


def params():
    return pltpu.CompilerParams(vmem_limit_bytes=VMEM)


def cost(flops, nbytes, trans=0):
    return pl.CostEstimate(flops=int(flops), bytes_accessed=int(nbytes), transcendentals=int(trans))


def split_planes(own_part, perm, kernel_id, chunks, shards, rows, after=()):
    _, slab_x, _, planes, full_y = own_part.shape
    half = planes // PAIR
    wide = full_y // shards
    span = perm.shape[0]
    sub = span // planes
    outs, specs, plan = [], [], []
    for order, _, first, slots in chunks:
        parts = ((0, half),) if order == "zy" else ((0,), (half,))
        for offsets in parts:
            count = slots * len(offsets)
            outs.append(jax.ShapeDtypeStruct((shards, count, slab_x, wide), jnp.bfloat16))
            specs.append(pl.BlockSpec((1, count, rows, wide), lambda s, i: (s, 0, i, 0)))
            plan.append([offset + first + j for offset in offsets for j in range(slots)])

    def body(part_ref, perm_ref, *refs):
        out_refs = refs[len(after) :]
        for b in range(rows // sub):
            block = part_ref[0, b * sub : (b + 1) * sub, 0].astype(jnp.float32)
            block = block.reshape(span, wide).astype(jnp.bfloat16)
            moved = jnp.dot(perm_ref[...], block, preferred_element_type=jnp.float32)
            moved = moved.astype(jnp.bfloat16).reshape(planes, sub, wide)
            for out_ref, slots_of in zip(out_refs, plan):
                for n, q in enumerate(slots_of):
                    out_ref[0, n, b * sub : (b + 1) * sub, :] = moved[q]

    return pl.pallas_call(
        body,
        grid=(shards, slab_x // rows),
        in_specs=[
            pl.BlockSpec((1, rows, 1, planes, wide), lambda s, i: (0, i, kernel_id, 0, s)),
            pl.BlockSpec(perm.shape, lambda s, i: (0, 0)),
        ]
        + [pl.BlockSpec(memory_space=pl.ANY)] * len(after),
        out_specs=specs,
        out_shape=outs,
        compiler_params=params(),
        cost_estimate=cost(0, 0),
        name="split_planes",
    )(own_part, perm, *after)


def hold(array, after):
    def body(*refs):
        del refs

    anywhere = pl.BlockSpec(memory_space=pl.ANY)
    return pl.pallas_call(
        body,
        in_specs=[anywhere] * (1 + len(after)),
        out_specs=anywhere,
        out_shape=jax.ShapeDtypeStruct(array.shape, array.dtype),
        input_output_aliases={0: 0},
        compiler_params=params(),
        cost_estimate=cost(0, 0),
        name="hold",
    )(array, *after)


def add_parts(a, b, after=()):
    shards, slots, slab_x, wide = a.shape

    def body(a_ref, b_ref, *refs):
        out_ref = refs[-1]
        out_ref[...] = (a_ref[...].astype(jnp.float32) + b_ref[...].astype(jnp.float32)).astype(jnp.bfloat16)

    spec = pl.BlockSpec((1, 1, slab_x, wide), lambda s, m: (s, m, 0, 0))
    return pl.pallas_call(
        body,
        grid=(shards, slots),
        in_specs=[spec, spec] + [pl.BlockSpec(memory_space=pl.ANY)] * len(after),
        out_specs=spec,
        out_shape=jax.ShapeDtypeStruct(a.shape, jnp.bfloat16),
        compiler_params=params(),
        cost_estimate=cost(a.size, 6 * a.size),
        name="add_parts",
    )(a, b, *after)


def scale(terms, lit, lit_pair, place, first, after=()):
    slots, slab_x, wide = terms[0].shape
    narrow = wide // PAIR
    count = len(terms)

    def body(place_ref, *refs):
        term_refs, (lit_ref, pair_ref) = refs[:count], refs[count : count + 2]
        out_ref, top_ref, bottom_ref = refs[-3:]
        left = place_ref[0] == 0
        for h in range(PAIR):
            total = term_refs[0][0, :, h * narrow : (h + 1) * narrow].astype(jnp.float32)
            for ref in term_refs[1:]:
                total = total + ref[0, :, h * narrow : (h + 1) * narrow].astype(jnp.float32)
            mine, theirs = lit_ref[0], pair_ref[0].astype(jnp.float32)
            by = jnp.where(left, mine, theirs) if h == 0 else jnp.where(left, theirs, mine)
            out_ref[0, :, h * narrow : (h + 1) * narrow] = (total / by).astype(jnp.bfloat16)
        top_ref[0] = out_ref[0, :BAND]
        bottom_ref[0] = out_ref[0, slab_x - BAND :]

    full = pl.BlockSpec((1, slab_x, wide), lambda m, place_ref: (m, 0, 0))
    edge = pl.BlockSpec((1, BAND, wide), lambda m, place_ref: (m, 0, 0))
    lit_spec = pl.BlockSpec((1, slab_x, narrow), lambda m, place_ref: (first + m, 0, 0))
    size = slots * slab_x * wide
    return pl.pallas_call(
        body,
        grid_spec=pltpu.PrefetchScalarGridSpec(
            num_scalar_prefetch=1,
            grid=(slots,),
            in_specs=[full] * count + [lit_spec, lit_spec] + [pl.BlockSpec(memory_space=pl.ANY)] * len(after),
            out_specs=[full, edge, edge],
        ),
        out_shape=[
            jax.ShapeDtypeStruct((slots, slab_x, wide), jnp.bfloat16),
            jax.ShapeDtypeStruct((slots, BAND, wide), jnp.bfloat16),
            jax.ShapeDtypeStruct((slots, BAND, wide), jnp.bfloat16),
        ],
        compiler_params=params(),
        cost_estimate=cost(size * 4, size * (2 * count + 6)),
        name="scale",
    )(place, *terms, lit, lit_pair, *after)


def band_tiles(length, widths, first, tiles, rows):
    shape = (widths.shape[0], tiles, rows, rows + 2 * BAND)
    base = first + rows * lax.broadcasted_iota(jnp.int32, shape, 1)
    row_pos = base + lax.broadcasted_iota(jnp.int32, shape, 2)
    col_pos = base - BAND + lax.broadcasted_iota(jnp.int32, shape, 3)
    offset = (row_pos - col_pos).astype(jnp.float32)
    inside = (jnp.abs(offset) <= BAND) & (col_pos >= 0) & (col_pos < length)
    distance = offset / (widths[:, None, None, None] * BAND)
    gaussian = jnp.where(inside, jnp.exp(-0.5 * distance * distance), jnp.float32(0.0))
    gaussian = gaussian / jnp.sum(gaussian, axis=3, keepdims=True)
    diagonal = jnp.where(offset == 0.0, jnp.float32(blend_weight), jnp.float32(0.0))
    return (gaussian + diagonal).astype(jnp.bfloat16)


def smooth_x(scaled, before, after, tiles_x, labels, first, behind=()):
    slots, slab_x, wide = scaled.shape
    classes, tiles, rows, window = tiles_x.shape

    def body(mid_ref, before_ref, after_ref, tiles_ref, label_ref, *refs):
        out_ref, low_ref, high_ref, cat_ref = refs[len(behind) :]
        cat_ref[:BAND] = before_ref[0]
        cat_ref[BAND : BAND + slab_x] = mid_ref[0]
        cat_ref[BAND + slab_x :] = after_ref[0]
        label = label_ref[0]
        for t in range(tiles):
            columns = cat_ref[t * rows : t * rows + window]
            total = jnp.dot(tiles_ref[0, t], columns, preferred_element_type=jnp.float32)
            for level in range(1, classes):
                product = jnp.dot(tiles_ref[level, t], columns, preferred_element_type=jnp.float32)
                total = jnp.where(label == level, product, total)
            bounded = (soft_bound * jnp.tanh(total / soft_bound)).astype(jnp.bfloat16)
            out_ref[0, t * rows : (t + 1) * rows] = bounded
            low_ref[0, t * rows : (t + 1) * rows] = bounded[:, :BAND]
            high_ref[0, t * rows : (t + 1) * rows] = bounded[:, wide - BAND :]

    full = pl.BlockSpec((1, slab_x, wide), lambda m: (m, 0, 0))
    edge = pl.BlockSpec((1, BAND, wide), lambda m: (m, 0, 0))
    side = pl.BlockSpec((1, slab_x, BAND), lambda m: (m, 0, 0))
    size = slots * slab_x * wide
    return pl.pallas_call(
        body,
        grid=(slots,),
        in_specs=[
            full,
            edge,
            edge,
            pl.BlockSpec(tiles_x.shape, lambda m: (0, 0, 0, 0)),
            pl.BlockSpec((1, 1, wide), lambda m: (first + m, 0, 0)),
        ]
        + [pl.BlockSpec(memory_space=pl.ANY)] * len(behind),
        out_specs=[full, side, side],
        out_shape=[
            jax.ShapeDtypeStruct((slots, slab_x, wide), jnp.bfloat16),
            jax.ShapeDtypeStruct((slots, slab_x, BAND), jnp.bfloat16),
            jax.ShapeDtypeStruct((slots, slab_x, BAND), jnp.bfloat16),
        ],
        scratch_shapes=[pltpu.VMEM((slab_x + 2 * BAND, wide), jnp.bfloat16)],
        compiler_params=params(),
        cost_estimate=cost(2 * classes * window * size, 6 * size, size),
        name="smooth_x",
    )(scaled, before, after, tiles_x, labels, *behind)


def smooth_y(bounded, before, after, tiles_y, labels, place, first, behind=()):
    slots, slab_x, wide = bounded.shape
    classes, tiles, window, narrow = tiles_y.shape

    def body(place_ref, mid_ref, before_ref, after_ref, tiles_ref, label_ref, *refs):
        keep_ref, send_ref, cat_ref = refs[len(behind) :]
        cat_ref[:, :BAND] = before_ref[0]
        cat_ref[:, BAND : BAND + wide] = mid_ref[0]
        cat_ref[:, BAND + wide :] = after_ref[0]
        label = label_ref[0]
        left = place_ref[0] == 0
        halves = []
        for t in range(tiles):
            columns = cat_ref[:, t * narrow : t * narrow + window]
            total = jnp.dot(columns, tiles_ref[0, t], preferred_element_type=jnp.float32)
            for level in range(1, classes):
                product = jnp.dot(columns, tiles_ref[level, t], preferred_element_type=jnp.float32)
                total = jnp.where(label == level, product, total)
            halves.append(total.astype(jnp.bfloat16))
        keep_ref[0] = jnp.where(left, halves[0], halves[1])
        send_ref[0] = jnp.where(left, halves[1], halves[0])

    full = pl.BlockSpec((1, slab_x, wide), lambda m, place_ref: (m, 0, 0))
    side = pl.BlockSpec((1, slab_x, BAND), lambda m, place_ref: (m, 0, 0))
    block = pl.BlockSpec((1, slab_x, narrow), lambda m, place_ref: (m, 0, 0))
    size = slots * slab_x * wide
    out = jax.ShapeDtypeStruct((slots, slab_x, narrow), jnp.bfloat16)
    return pl.pallas_call(
        body,
        grid_spec=pltpu.PrefetchScalarGridSpec(
            num_scalar_prefetch=1,
            grid=(slots,),
            in_specs=[
                full,
                side,
                side,
                pl.BlockSpec(tiles_y.shape, lambda m, place_ref: (0, 0, 0, 0)),
                pl.BlockSpec((1, slab_x, 1), lambda m, place_ref: (first + m, 0, 0)),
            ]
            + [pl.BlockSpec(memory_space=pl.ANY)] * len(behind),
            out_specs=[block, block],
            scratch_shapes=[pltpu.VMEM((slab_x, wide + 2 * BAND), jnp.bfloat16)],
        ),
        out_shape=[out, out],
        compiler_params=params(),
        cost_estimate=cost(2 * classes * window * size, 6 * size),
        name="smooth_y",
    )(place, bounded, before, after, tiles_y, labels, *behind)


def join_planes(kept, came, perm_back, slots_of, planes, rows):
    _, slab_x, narrow = kept[0].shape
    span = perm_back.shape[0]
    sub = span // planes
    half = planes // PAIR
    kernels = len(slots_of) // half
    count = len(kept)

    def body(*refs):
        kept_refs, came_refs = refs[:count], refs[count : 2 * count]
        perm_ref, out_ref, stack_ref = refs[2 * count :]
        for k in range(kernels):
            for b in range(rows // sub):
                for j in range(half):
                    c, m = slots_of[k * half + j]
                    at = slice(b * sub, (b + 1) * sub)
                    stack_ref[j * sub : (j + 1) * sub] = kept_refs[c][m, at]
                    stack_ref[(half + j) * sub : (half + j + 1) * sub] = came_refs[c][m, at]
                moved = jnp.dot(perm_ref[...], stack_ref[...], preferred_element_type=jnp.float32)
                moved = moved.reshape(sub, planes, narrow).astype(jnp.bfloat16)
                out_ref[b * sub : (b + 1) * sub, k] = moved

    specs = [pl.BlockSpec((a.shape[0], rows, narrow), lambda i: (0, i, 0)) for a in kept]
    size = slab_x * kernels * planes * narrow
    return pl.pallas_call(
        body,
        grid=(slab_x // rows,),
        in_specs=specs + specs + [pl.BlockSpec(perm_back.shape, lambda i: (0, 0))],
        out_specs=pl.BlockSpec((rows, kernels, planes, narrow), lambda i: (i, 0, 0, 0)),
        out_shape=jax.ShapeDtypeStruct((slab_x, kernels, planes, narrow), jnp.bfloat16),
        scratch_shapes=[pltpu.VMEM((span, narrow), jnp.bfloat16)],
        compiler_params=params(),
        cost_estimate=cost(2 * span * size, 4 * size),
        name="join_planes",
    )(*kept, *came, perm_back)


def per_device(partial_kernels, illumination, classes_x, classes_y, widths_x, widths_y):
    _, slab_x, kernels, planes, full_y = partial_kernels.shape
    groups = lax.axis_size("ev")
    owners = lax.axis_size("gx")
    slab_y = full_y // groups
    full_x = slab_x * owners
    shards = groups // PAIR
    half = planes // PAIR
    me = lax.axis_index("ev")
    pair = lax.rem(me, PAIR)
    line = me // PAIR
    place = pair.astype(jnp.int32).reshape(1)

    other = [(i, i ^ 1) for i in range(groups)]
    z_up = [(i, i + PAIR) for i in range(groups - PAIR)]
    z_down = [(b, a) for a, b in z_up]
    x_up = [(i, i + 1) for i in range(owners - 1)]
    x_down = [(b, a) for a, b in x_up]
    lines = [[z * PAIR + y for z in range(shards)] for y in range(PAIR)]

    def over_line(parts):
        return lax.psum_scatter(
            parts, "ev", scatter_dimension=0, axis_index_groups=lines, tiled=True
        ).reshape(parts.shape[1:])

    sub = 256 // planes
    span = sub * planes
    to_row = lax.broadcasted_iota(jnp.int32, (span, span), 0)
    from_row = lax.broadcasted_iota(jnp.int32, (span, span), 1)
    plane_of = lax.rem(to_row // sub + half * pair, planes)
    perm = (from_row == lax.rem(to_row, sub) * planes + plane_of).astype(jnp.bfloat16)
    chunks = plan_chunks(kernels, half)

    lit_planes = jnp.transpose(illumination, (1, 0, 2))
    lit = lax.dynamic_slice_in_dim(lit_planes, half * pair, half, 0)
    lit_sent = lax.dynamic_slice_in_dim(lit_planes, half * (1 - pair), half, 0).astype(jnp.bfloat16)

    lit_pair = lax.ppermute(lit_sent, "ev", other)
    split, before = {}, []
    for some in (chunks[:1], chunks[1:2], chunks[2:]):
        for k in range(kernels):
            mine = [c for c in some if c[1] == k]
            if mine:
                arrays = list(split_planes(partial_kernels, perm, k, mine, shards, slab_x, before))
                before = arrays[:1]
                for c in mine:
                    split[c] = (arrays.pop(0),) if c[0] == "zy" else (arrays.pop(0), arrays.pop(0))

    labels_mine = lax.dynamic_slice_in_dim(classes_x, half * pair, half, 0)
    labels_sent = lax.dynamic_slice_in_dim(classes_x, half * (1 - pair), half, 0)
    labels_pair = lax.ppermute(labels_sent, "ev", other)
    labels_x = jnp.where(
        pair == 0,
        jnp.concatenate([labels_mine, labels_pair], 1),
        jnp.concatenate([labels_pair, labels_mine], 1),
    ).reshape(half, 1, PAIR * slab_y)
    labels_y = lax.dynamic_slice_in_dim(classes_y.T, half * pair, half, 0).reshape(half, slab_x, 1)

    tile = min(256, slab_x)
    tiles_x = band_tiles(full_x, widths_x, lax.axis_index("gx") * slab_x, slab_x // tile, tile)
    tiles_y = jnp.swapaxes(band_tiles(full_y, widths_y, line * PAIR * slab_y, PAIR, slab_y), 2, 3)

    slots_of, added, sums, kept, came = {}, {}, {}, {}, {}
    for n, (order, k, first, slots) in enumerate(chunks):
        for m in range(slots):
            slots_of[k * half + first + m] = (n, m)

    def begin(n, after=(), behind=()):
        order, k, first, slots = chunks[n]
        if order == "yz":
            own, sent = split[chunks[n]]
            if behind:
                sent = hold(sent, behind)
            added[n] = add_parts(own, lax.ppermute(sent, "ev", other), after)
            sums[n] = [over_line(added[n])]
        else:
            both = over_line(split[chunks[n]][0])
            sums[n] = [both[:slots], lax.ppermute(both[slots:], "ev", other)]

    scaled, sides = {}, {}

    def divide(n, after=()):
        order, k, first, slots = chunks[n]
        scaled[n], top, bottom = scale(sums[n], lit, lit_pair, place, first, after)
        sides[n] = lax.ppermute(bottom, "gx", x_up), lax.ppermute(top, "gx", x_down)

    bounded, ends = {}, {}

    def cross_x(n, after=()):
        order, k, first, slots = chunks[n]
        bounded[n], low, high = smooth_x(scaled[n], *sides[n], tiles_x, labels_x, first, after)
        ends[n] = lax.ppermute(high, "ev", z_up), lax.ppermute(low, "ev", z_down)

    def cross_y(n, after=()):
        order, k, first, slots = chunks[n]
        kept[n], send = smooth_y(bounded[n], *ends[n], tiles_y, labels_y, place, first, after)
        came[n] = lax.ppermute(send, "ev", other)

    last = len(chunks)
    begin(0)
    begin(1, [split[c][0] for c in chunks[2:]], [lit_pair, labels_pair])
    begin(2, [sums[0][0]])
    divide(1)
    cross_x(1)
    cross_y(1)
    begin(3, [kept[1], sums[0][1]])
    divide(0)
    cross_x(0)
    cross_y(0)
    for n in range(4, last):
        begin(n, [kept[0]])
    divide(2)
    divide(3, [came[1]])
    cross_x(2, [scaled[3]])
    cross_x(3)
    cross_y(2, [bounded[3]])
    cross_y(3)
    for n in range(4, last):
        divide(n, [kept[n - 1], came[0], came[2]])
        cross_x(n)
        cross_y(n)
    order = range(last)
    return join_planes([kept[n] for n in order], [came[n] for n in order], perm.T, slots_of, planes, slab_x // 2)


def solution(mesh):
    return jax.shard_map(
        per_device,
        mesh=mesh,
        in_specs=(
            P("ev", "gx", None, None, None),
            P("gx", None, "ev"),
            P(None, "ev"),
            P("gx", None),
            P(),
            P(),
        ),
        out_specs=P("gx", None, None, "ev"),
        check_vma=False,
    )
```

```python
import functools

import jax
import jax.numpy as jnp
from jax import lax
from jax.experimental import pallas as pl
from jax.experimental.pallas import tpu as pltpu
from jax.sharding import PartitionSpec as P

BAND = 128
PAIR = 2

blend_weight = 0.25
soft_bound = 2.0


def plan_chunks(kernels, half):
    lead = half // 2
    chunks = [("zy", 0, 0, lead), ("yz", 0, lead, half - lead)]
    for k in range(1, kernels):
        chunks.append(("yz", k, 0, lead))
        chunks += [("yz", k, j, 1) for j in range(lead, half)]
    return chunks


VMEM = 64 * 1024 * 1024


def params():
    return pltpu.CompilerParams(vmem_limit_bytes=VMEM)


def cost(flops, nbytes, trans=0):
    return pl.CostEstimate(flops=int(flops), bytes_accessed=int(nbytes), transcendentals=int(trans))


def split_planes(own_part, perm, kernel_id, chunks, shards, rows, after=()):
    _, slab_x, _, planes, full_y = own_part.shape
    half = planes // PAIR
    wide = full_y // shards
    span = perm.shape[0]
    sub = span // planes
    outs, specs, plan = [], [], []
    for order, _, first, slots in chunks:
        parts = ((0, half),) if order == "zy" else ((0,), (half,))
        for offsets in parts:
            count = slots * len(offsets)
            outs.append(jax.ShapeDtypeStruct((shards, count, slab_x, wide), jnp.bfloat16))
            specs.append(pl.BlockSpec((1, count, rows, wide), lambda s, i: (s, 0, i, 0)))
            plan.append([offset + first + j for offset in offsets for j in range(slots)])

    def body(part_ref, perm_ref, *refs):
        out_refs = refs[len(after) :]
        for b in range(rows // sub):
            block = part_ref[0, b * sub : (b + 1) * sub, 0].astype(jnp.float32)
            block = block.reshape(span, wide).astype(jnp.bfloat16)
            moved = jnp.dot(perm_ref[...], block, preferred_element_type=jnp.float32)
            moved = moved.astype(jnp.bfloat16).reshape(planes, sub, wide)
            for out_ref, slots_of in zip(out_refs, plan):
                for n, q in enumerate(slots_of):
                    out_ref[0, n, b * sub : (b + 1) * sub, :] = moved[q]

    return pl.pallas_call(
        body,
        grid=(shards, slab_x // rows),
        in_specs=[
            pl.BlockSpec((1, rows, 1, planes, wide), lambda s, i: (0, i, kernel_id, 0, s)),
            pl.BlockSpec(perm.shape, lambda s, i: (0, 0)),
        ]
        + [pl.BlockSpec(memory_space=pl.ANY)] * len(after),
        out_specs=specs,
        out_shape=outs,
        compiler_params=params(),
        cost_estimate=cost(0, 0),
        name="split_planes",
    )(own_part, perm, *after)


def hold(array, after):
    def body(*refs):
        del refs

    anywhere = pl.BlockSpec(memory_space=pl.ANY)
    return pl.pallas_call(
        body,
        in_specs=[anywhere] * (1 + len(after)),
        out_specs=anywhere,
        out_shape=jax.ShapeDtypeStruct(array.shape, array.dtype),
        input_output_aliases={0: 0},
        compiler_params=params(),
        cost_estimate=cost(0, 0),
        name="hold",
    )(array, *after)


def add_parts(a, b, after=()):
    shards, slots, slab_x, wide = a.shape

    def body(a_ref, b_ref, *refs):
        out_ref = refs[-1]
        out_ref[...] = (a_ref[...].astype(jnp.float32) + b_ref[...].astype(jnp.float32)).astype(jnp.bfloat16)

    spec = pl.BlockSpec((1, 1, slab_x, wide), lambda s, m: (s, m, 0, 0))
    return pl.pallas_call(
        body,
        grid=(shards, slots),
        in_specs=[spec, spec] + [pl.BlockSpec(memory_space=pl.ANY)] * len(after),
        out_specs=spec,
        out_shape=jax.ShapeDtypeStruct(a.shape, jnp.bfloat16),
        compiler_params=params(),
        cost_estimate=cost(a.size, 6 * a.size),
        name="add_parts",
    )(a, b, *after)


def scale(terms, lit, lit_pair, place, first, after=()):
    slots, slab_x, wide = terms[0].shape
    narrow = wide // PAIR
    count = len(terms)

    def body(place_ref, *refs):
        term_refs, (lit_ref, pair_ref) = refs[:count], refs[count : count + 2]
        out_ref, top_ref, bottom_ref = refs[-3:]
        left = place_ref[0] == 0
        for h in range(PAIR):
            total = term_refs[0][0, :, h * narrow : (h + 1) * narrow].astype(jnp.float32)
            for ref in term_refs[1:]:
                total = total + ref[0, :, h * narrow : (h + 1) * narrow].astype(jnp.float32)
            mine, theirs = lit_ref[0], pair_ref[0].astype(jnp.float32)
            by = jnp.where(left, mine, theirs) if h == 0 else jnp.where(left, theirs, mine)
            out_ref[0, :, h * narrow : (h + 1) * narrow] = (total / by).astype(jnp.bfloat16)
        top_ref[0] = out_ref[0, :BAND]
        bottom_ref[0] = out_ref[0, slab_x - BAND :]

    full = pl.BlockSpec((1, slab_x, wide), lambda m, place_ref: (m, 0, 0))
    edge = pl.BlockSpec((1, BAND, wide), lambda m, place_ref: (m, 0, 0))
    lit_spec = pl.BlockSpec((1, slab_x, narrow), lambda m, place_ref: (first + m, 0, 0))
    size = slots * slab_x * wide
    return pl.pallas_call(
        body,
        grid_spec=pltpu.PrefetchScalarGridSpec(
            num_scalar_prefetch=1,
            grid=(slots,),
            in_specs=[full] * count + [lit_spec, lit_spec] + [pl.BlockSpec(memory_space=pl.ANY)] * len(after),
            out_specs=[full, edge, edge],
        ),
        out_shape=[
            jax.ShapeDtypeStruct((slots, slab_x, wide), jnp.bfloat16),
            jax.ShapeDtypeStruct((slots, BAND, wide), jnp.bfloat16),
            jax.ShapeDtypeStruct((slots, BAND, wide), jnp.bfloat16),
        ],
        compiler_params=params(),
        cost_estimate=cost(size * 4, size * (2 * count + 6)),
        name="scale",
    )(place, *terms, lit, lit_pair, *after)


def band_tiles(length, widths, first, tiles, rows):
    shape = (widths.shape[0], tiles, rows, rows + 2 * BAND)
    base = first + rows * lax.broadcasted_iota(jnp.int32, shape, 1)
    row_pos = base + lax.broadcasted_iota(jnp.int32, shape, 2)
    col_pos = base - BAND + lax.broadcasted_iota(jnp.int32, shape, 3)
    offset = (row_pos - col_pos).astype(jnp.float32)
    inside = (jnp.abs(offset) <= BAND) & (col_pos >= 0) & (col_pos < length)
    distance = offset / (widths[:, None, None, None] * BAND)
    gaussian = jnp.where(inside, jnp.exp(-0.5 * distance * distance), jnp.float32(0.0))
    gaussian = gaussian / jnp.sum(gaussian, axis=3, keepdims=True)
    diagonal = jnp.where(offset == 0.0, jnp.float32(blend_weight), jnp.float32(0.0))
    return (gaussian + diagonal).astype(jnp.bfloat16)


def smooth_x(scaled, before, after, tiles_x, labels, first, behind=()):
    slots, slab_x, wide = scaled.shape
    classes, tiles, rows, window = tiles_x.shape

    def body(mid_ref, before_ref, after_ref, tiles_ref, label_ref, *refs):
        out_ref, low_ref, high_ref, cat_ref = refs[len(behind) :]
        cat_ref[:BAND] = before_ref[0]
        cat_ref[BAND : BAND + slab_x] = mid_ref[0]
        cat_ref[BAND + slab_x :] = after_ref[0]
        label = label_ref[0]
        for t in range(tiles):
            columns = cat_ref[t * rows : t * rows + window]
            total = jnp.dot(tiles_ref[0, t], columns, preferred_element_type=jnp.float32)
            for level in range(1, classes):
                product = jnp.dot(tiles_ref[level, t], columns, preferred_element_type=jnp.float32)
                total = jnp.where(label == level, product, total)
            bounded = (soft_bound * jnp.tanh(total / soft_bound)).astype(jnp.bfloat16)
            out_ref[0, t * rows : (t + 1) * rows] = bounded
            low_ref[0, t * rows : (t + 1) * rows] = bounded[:, :BAND]
            high_ref[0, t * rows : (t + 1) * rows] = bounded[:, wide - BAND :]

    full = pl.BlockSpec((1, slab_x, wide), lambda m: (m, 0, 0))
    edge = pl.BlockSpec((1, BAND, wide), lambda m: (m, 0, 0))
    side = pl.BlockSpec((1, slab_x, BAND), lambda m: (m, 0, 0))
    size = slots * slab_x * wide
    return pl.pallas_call(
        body,
        grid=(slots,),
        in_specs=[
            full,
            edge,
            edge,
            pl.BlockSpec(tiles_x.shape, lambda m: (0, 0, 0, 0)),
            pl.BlockSpec((1, 1, wide), lambda m: (first + m, 0, 0)),
        ]
        + [pl.BlockSpec(memory_space=pl.ANY)] * len(behind),
        out_specs=[full, side, side],
        out_shape=[
            jax.ShapeDtypeStruct((slots, slab_x, wide), jnp.bfloat16),
            jax.ShapeDtypeStruct((slots, slab_x, BAND), jnp.bfloat16),
            jax.ShapeDtypeStruct((slots, slab_x, BAND), jnp.bfloat16),
        ],
        scratch_shapes=[pltpu.VMEM((slab_x + 2 * BAND, wide), jnp.bfloat16)],
        compiler_params=params(),
        cost_estimate=cost(2 * classes * window * size, 6 * size, size),
        name="smooth_x",
    )(scaled, before, after, tiles_x, labels, *behind)


def smooth_y(bounded, before, after, tiles_y, labels, place, first, behind=()):
    slots, slab_x, wide = bounded.shape
    classes, tiles, window, narrow = tiles_y.shape

    def body(place_ref, mid_ref, before_ref, after_ref, tiles_ref, label_ref, *refs):
        keep_ref, send_ref, cat_ref = refs[len(behind) :]
        cat_ref[:, :BAND] = before_ref[0]
        cat_ref[:, BAND : BAND + wide] = mid_ref[0]
        cat_ref[:, BAND + wide :] = after_ref[0]
        label = label_ref[0]
        left = place_ref[0] == 0
        halves = []
        for t in range(tiles):
            columns = cat_ref[:, t * narrow : t * narrow + window]
            total = jnp.dot(columns, tiles_ref[0, t], preferred_element_type=jnp.float32)
            for level in range(1, classes):
                product = jnp.dot(columns, tiles_ref[level, t], preferred_element_type=jnp.float32)
                total = jnp.where(label == level, product, total)
            halves.append(total.astype(jnp.bfloat16))
        keep_ref[0] = jnp.where(left, halves[0], halves[1])
        send_ref[0] = jnp.where(left, halves[1], halves[0])

    full = pl.BlockSpec((1, slab_x, wide), lambda m, place_ref: (m, 0, 0))
    side = pl.BlockSpec((1, slab_x, BAND), lambda m, place_ref: (m, 0, 0))
    block = pl.BlockSpec((1, slab_x, narrow), lambda m, place_ref: (m, 0, 0))
    size = slots * slab_x * wide
    out = jax.ShapeDtypeStruct((slots, slab_x, narrow), jnp.bfloat16)
    return pl.pallas_call(
        body,
        grid_spec=pltpu.PrefetchScalarGridSpec(
            num_scalar_prefetch=1,
            grid=(slots,),
            in_specs=[
                full,
                side,
                side,
                pl.BlockSpec(tiles_y.shape, lambda m, place_ref: (0, 0, 0, 0)),
                pl.BlockSpec((1, slab_x, 1), lambda m, place_ref: (first + m, 0, 0)),
            ]
            + [pl.BlockSpec(memory_space=pl.ANY)] * len(behind),
            out_specs=[block, block],
            scratch_shapes=[pltpu.VMEM((slab_x, wide + 2 * BAND), jnp.bfloat16)],
        ),
        out_shape=[out, out],
        compiler_params=params(),
        cost_estimate=cost(2 * classes * window * size, 6 * size),
        name="smooth_y",
    )(place, bounded, before, after, tiles_y, labels, *behind)


def join_planes(kept, came, perm_back, slots_of, planes, kernels, kernel_id, rows, base=()):
    _, slab_x, narrow = kept[0].shape
    span = perm_back.shape[0]
    sub = span // planes
    half = planes // PAIR
    count = len(kept)

    def body(*refs):
        kept_refs, came_refs = refs[:count], refs[count : 2 * count]
        perm_ref = refs[2 * count]
        out_ref, stack_ref = refs[-2:]
        for b in range(rows // sub):
            at = slice(b * sub, (b + 1) * sub)
            for j in range(half):
                c, m = slots_of[j]
                stack_ref[j * sub : (j + 1) * sub] = kept_refs[c][m, at]
                stack_ref[(half + j) * sub : (half + j + 1) * sub] = came_refs[c][m, at]
            moved = jnp.dot(perm_ref[...], stack_ref[...], preferred_element_type=jnp.float32)
            out_ref[at, 0] = moved.reshape(sub, planes, narrow).astype(jnp.bfloat16)

    specs = [pl.BlockSpec((a.shape[0], rows, narrow), lambda i: (0, i, 0)) for a in kept]
    size = slab_x * planes * narrow
    return pl.pallas_call(
        body,
        grid=(slab_x // rows,),
        in_specs=specs
        + specs
        + [pl.BlockSpec(perm_back.shape, lambda i: (0, 0))]
        + [pl.BlockSpec(memory_space=pl.ANY)] * len(base),
        out_specs=pl.BlockSpec((rows, 1, planes, narrow), lambda i: (i, kernel_id, 0, 0)),
        out_shape=jax.ShapeDtypeStruct((slab_x, kernels, planes, narrow), jnp.bfloat16),
        scratch_shapes=[pltpu.VMEM((span, narrow), jnp.bfloat16)],
        input_output_aliases={2 * count + 1: 0} if base else {},
        compiler_params=params(),
        cost_estimate=cost(2 * span * size, 4 * size),
        name="join_planes",
    )(*kept, *came, perm_back, *base)


def per_device(partial_kernels, illumination, classes_x, classes_y, widths_x, widths_y):
    _, slab_x, kernels, planes, full_y = partial_kernels.shape
    groups = lax.axis_size("ev")
    owners = lax.axis_size("gx")
    slab_y = full_y // groups
    full_x = slab_x * owners
    shards = groups // PAIR
    half = planes // PAIR
    me = lax.axis_index("ev")
    pair = lax.rem(me, PAIR)
    line = me // PAIR
    place = pair.astype(jnp.int32).reshape(1)

    other = [(i, i ^ 1) for i in range(groups)]
    z_up = [(i, i + PAIR) for i in range(groups - PAIR)]
    z_down = [(b, a) for a, b in z_up]
    x_up = [(i, i + 1) for i in range(owners - 1)]
    x_down = [(b, a) for a, b in x_up]
    lines = [[z * PAIR + y for z in range(shards)] for y in range(PAIR)]

    def over_line(parts):
        return lax.psum_scatter(
            parts, "ev", scatter_dimension=0, axis_index_groups=lines, tiled=True
        ).reshape(parts.shape[1:])

    sub = 256 // planes
    span = sub * planes
    to_row = lax.broadcasted_iota(jnp.int32, (span, span), 0)
    from_row = lax.broadcasted_iota(jnp.int32, (span, span), 1)
    plane_of = lax.rem(to_row // sub + half * pair, planes)
    perm = (from_row == lax.rem(to_row, sub) * planes + plane_of).astype(jnp.bfloat16)
    chunks = plan_chunks(kernels, half)

    lit_planes = jnp.transpose(illumination, (1, 0, 2))
    lit = lax.dynamic_slice_in_dim(lit_planes, half * pair, half, 0)
    lit_sent = lax.dynamic_slice_in_dim(lit_planes, half * (1 - pair), half, 0).astype(jnp.bfloat16)

    lit_pair = lax.ppermute(lit_sent, "ev", other)
    split, before = {}, []
    for some in (chunks[:1], chunks[1:2], chunks[2:]):
        for k in range(kernels):
            mine = [c for c in some if c[1] == k]
            if mine:
                arrays = list(split_planes(partial_kernels, perm, k, mine, shards, slab_x, before))
                before = arrays[:1]
                for c in mine:
                    split[c] = (arrays.pop(0),) if c[0] == "zy" else (arrays.pop(0), arrays.pop(0))

    labels_mine = lax.dynamic_slice_in_dim(classes_x, half * pair, half, 0)
    labels_sent = lax.dynamic_slice_in_dim(classes_x, half * (1 - pair), half, 0)
    labels_pair = lax.ppermute(labels_sent, "ev", other)
    labels_x = jnp.where(
        pair == 0,
        jnp.concatenate([labels_mine, labels_pair], 1),
        jnp.concatenate([labels_pair, labels_mine], 1),
    ).reshape(half, 1, PAIR * slab_y)
    labels_y = lax.dynamic_slice_in_dim(classes_y.T, half * pair, half, 0).reshape(half, slab_x, 1)

    tile = min(256, slab_x)
    tiles_x = band_tiles(full_x, widths_x, lax.axis_index("gx") * slab_x, slab_x // tile, tile)
    tiles_y = jnp.swapaxes(band_tiles(full_y, widths_y, line * PAIR * slab_y, PAIR, slab_y), 2, 3)

    slots_of, added, sums, kept, came = {}, {}, {}, {}, {}
    for n, (order, k, first, slots) in enumerate(chunks):
        for m in range(slots):
            slots_of[k * half + first + m] = (n, m)

    def begin(n, after=(), behind=()):
        order, k, first, slots = chunks[n]
        if order == "yz":
            own, sent = split[chunks[n]]
            if behind:
                sent = hold(sent, behind)
            added[n] = add_parts(own, lax.ppermute(sent, "ev", other), after)
            sums[n] = [over_line(added[n])]
        else:
            both = over_line(split[chunks[n]][0])
            sums[n] = [both[:slots], lax.ppermute(both[slots:], "ev", other)]

    scaled, sides = {}, {}

    def divide(n, after=()):
        order, k, first, slots = chunks[n]
        scaled[n], top, bottom = scale(sums[n], lit, lit_pair, place, first, after)
        sides[n] = lax.ppermute(bottom, "gx", x_up), lax.ppermute(top, "gx", x_down)

    bounded, ends = {}, {}

    def cross_x(n, after=()):
        order, k, first, slots = chunks[n]
        bounded[n], low, high = smooth_x(scaled[n], *sides[n], tiles_x, labels_x, first, after)
        ends[n] = lax.ppermute(high, "ev", z_up), lax.ppermute(low, "ev", z_down)

    def cross_y(n, after=()):
        order, k, first, slots = chunks[n]
        kept[n], send = smooth_y(bounded[n], *ends[n], tiles_y, labels_y, place, first, after)
        came[n] = lax.ppermute(send, "ev", other)

    last = len(chunks)
    begin(0)
    begin(1, [split[c][0] for c in chunks[2:]], [lit_pair, labels_pair])
    begin(2, [sums[0][0]])
    divide(1)
    cross_x(1)
    cross_y(1)
    begin(3, [kept[1], sums[0][1]])
    divide(0)
    cross_x(0)
    cross_y(0)
    for n in range(4, last):
        begin(n, [kept[0]])
    divide(2)
    divide(3, [came[1]])
    cross_x(2, [scaled[3]])
    cross_x(3)
    cross_y(2, [bounded[3]])
    cross_y(3)
    for n in range(4, last):
        divide(n, [kept[n - 1], came[0], came[2]])
        cross_x(n)
        cross_y(n)
    base = ()
    for k in range(kernels):
        mine = [n for n in range(last) if chunks[n][1] == k]
        where = [slots_of[k * half + j] for j in range(half)]
        where = [(mine.index(n), m) for n, m in where]
        parts = [kept[n] for n in mine], [came[n] for n in mine]
        base = (join_planes(*parts, perm.T, where, planes, kernels, k, slab_x // 2, base),)
    return base[0]


def solution(mesh):
    return jax.shard_map(
        per_device,
        mesh=mesh,
        in_specs=(
            P("ev", "gx", None, None, None),
            P("gx", None, "ev"),
            P(None, "ev"),
            P("gx", None),
            P(),
            P(),
        ),
        out_specs=P("gx", None, None, "ev"),
        check_vma=False,
    )
```

```python
import functools

import jax
import jax.numpy as jnp
from jax import lax
from jax.experimental import pallas as pl
from jax.experimental.pallas import tpu as pltpu
from jax.sharding import PartitionSpec as P

BAND = 128
PAIR = 2

blend_weight = 0.25
soft_bound = 2.0


def plan_chunks(kernels, half):
    lead = half // 2
    chunks = [("zy", 0, 0, lead), ("yz", 0, lead, half - lead)]
    for k in range(1, kernels):
        chunks.append(("yz", k, 0, lead))
        chunks += [("yz", k, j, 1) for j in range(lead, half)]
    return chunks


VMEM = 64 * 1024 * 1024


def params():
    return pltpu.CompilerParams(vmem_limit_bytes=VMEM)


def cost(flops, nbytes, trans=0):
    return pl.CostEstimate(flops=int(flops), bytes_accessed=int(nbytes), transcendentals=int(trans))


def split_planes(own_part, perm, kernel_id, chunks, shards, rows, after=()):
    _, slab_x, _, planes, full_y = own_part.shape
    half = planes // PAIR
    wide = full_y // shards
    span = perm.shape[0]
    sub = span // planes
    outs, specs, plan = [], [], []
    for order, _, first, slots in chunks:
        parts = ((0, half),) if order == "zy" else ((0,), (half,))
        for offsets in parts:
            count = slots * len(offsets)
            outs.append(jax.ShapeDtypeStruct((shards, count, slab_x, wide), jnp.bfloat16))
            specs.append(pl.BlockSpec((1, count, rows, wide), lambda s, i: (s, 0, i, 0)))
            plan.append([offset + first + j for offset in offsets for j in range(slots)])

    used = [q for slots_of in plan for q in slots_of]
    perm = jnp.concatenate([perm[q * sub : (q + 1) * sub] for q in used])

    def body(part_ref, perm_ref, *refs):
        out_refs = refs[len(after) :]
        for b in range(rows // sub):
            block = part_ref[0, b * sub : (b + 1) * sub, 0].astype(jnp.float32)
            block = block.reshape(span, wide).astype(jnp.bfloat16)
            moved = jnp.dot(perm_ref[...], block, preferred_element_type=jnp.float32)
            moved = moved.astype(jnp.bfloat16).reshape(len(used), sub, wide)
            at = 0
            for out_ref, slots_of in zip(out_refs, plan):
                for n in range(len(slots_of)):
                    out_ref[0, n, b * sub : (b + 1) * sub, :] = moved[at + n]
                at += len(slots_of)

    return pl.pallas_call(
        body,
        grid=(shards, slab_x // rows),
        in_specs=[
            pl.BlockSpec((1, rows, 1, planes, wide), lambda s, i: (0, i, kernel_id, 0, s)),
            pl.BlockSpec(perm.shape, lambda s, i: (0, 0)),
        ]
        + [pl.BlockSpec(memory_space=pl.ANY)] * len(after),
        out_specs=specs,
        out_shape=outs,
        compiler_params=params(),
        cost_estimate=cost(0, 0),
        name="split_planes",
    )(own_part, perm, *after)


def hold(array, after):
    def body(*refs):
        del refs

    anywhere = pl.BlockSpec(memory_space=pl.ANY)
    return pl.pallas_call(
        body,
        in_specs=[anywhere] * (1 + len(after)),
        out_specs=anywhere,
        out_shape=jax.ShapeDtypeStruct(array.shape, array.dtype),
        input_output_aliases={0: 0},
        compiler_params=params(),
        cost_estimate=cost(0, 0),
        name="hold",
    )(array, *after)


def add_parts(a, b, after=()):
    shards, slots, slab_x, wide = a.shape

    def body(a_ref, b_ref, *refs):
        out_ref = refs[-1]
        out_ref[...] = (a_ref[...].astype(jnp.float32) + b_ref[...].astype(jnp.float32)).astype(jnp.bfloat16)

    spec = pl.BlockSpec((1, 1, slab_x, wide), lambda s, m: (s, m, 0, 0))
    return pl.pallas_call(
        body,
        grid=(shards, slots),
        in_specs=[spec, spec] + [pl.BlockSpec(memory_space=pl.ANY)] * len(after),
        out_specs=spec,
        out_shape=jax.ShapeDtypeStruct(a.shape, jnp.bfloat16),
        compiler_params=params(),
        cost_estimate=cost(a.size, 6 * a.size),
        name="add_parts",
    )(a, b, *after)


def scale(terms, lit, lit_pair, place, first, after=()):
    slots, slab_x, wide = terms[0].shape
    narrow = wide // PAIR
    count = len(terms)

    def body(place_ref, *refs):
        term_refs, (lit_ref, pair_ref) = refs[:count], refs[count : count + 2]
        out_ref, top_ref, bottom_ref = refs[-3:]
        left = place_ref[0] == 0
        for h in range(PAIR):
            total = term_refs[0][0, :, h * narrow : (h + 1) * narrow].astype(jnp.float32)
            for ref in term_refs[1:]:
                total = total + ref[0, :, h * narrow : (h + 1) * narrow].astype(jnp.float32)
            mine, theirs = lit_ref[0], pair_ref[0].astype(jnp.float32)
            by = jnp.where(left, mine, theirs) if h == 0 else jnp.where(left, theirs, mine)
            out_ref[0, :, h * narrow : (h + 1) * narrow] = (total / by).astype(jnp.bfloat16)
        top_ref[0] = out_ref[0, :BAND]
        bottom_ref[0] = out_ref[0, slab_x - BAND :]

    full = pl.BlockSpec((1, slab_x, wide), lambda m, place_ref: (m, 0, 0))
    edge = pl.BlockSpec((1, BAND, wide), lambda m, place_ref: (m, 0, 0))
    lit_spec = pl.BlockSpec((1, slab_x, narrow), lambda m, place_ref: (first + m, 0, 0))
    size = slots * slab_x * wide
    return pl.pallas_call(
        body,
        grid_spec=pltpu.PrefetchScalarGridSpec(
            num_scalar_prefetch=1,
            grid=(slots,),
            in_specs=[full] * count + [lit_spec, lit_spec] + [pl.BlockSpec(memory_space=pl.ANY)] * len(after),
            out_specs=[full, edge, edge],
        ),
        out_shape=[
            jax.ShapeDtypeStruct((slots, slab_x, wide), jnp.bfloat16),
            jax.ShapeDtypeStruct((slots, BAND, wide), jnp.bfloat16),
            jax.ShapeDtypeStruct((slots, BAND, wide), jnp.bfloat16),
        ],
        compiler_params=params(),
        cost_estimate=cost(size * 4, size * (2 * count + 6)),
        name="scale",
    )(place, *terms, lit, lit_pair, *after)


def band_tiles(length, widths, first, tiles, rows):
    shape = (widths.shape[0], tiles, rows, rows + 2 * BAND)
    base = first + rows * lax.broadcasted_iota(jnp.int32, shape, 1)
    row_pos = base + lax.broadcasted_iota(jnp.int32, shape, 2)
    col_pos = base - BAND + lax.broadcasted_iota(jnp.int32, shape, 3)
    offset = (row_pos - col_pos).astype(jnp.float32)
    inside = (jnp.abs(offset) <= BAND) & (col_pos >= 0) & (col_pos < length)
    distance = offset / (widths[:, None, None, None] * BAND)
    gaussian = jnp.where(inside, jnp.exp(-0.5 * distance * distance), jnp.float32(0.0))
    gaussian = gaussian / jnp.sum(gaussian, axis=3, keepdims=True)
    diagonal = jnp.where(offset == 0.0, jnp.float32(blend_weight), jnp.float32(0.0))
    return (gaussian + diagonal).astype(jnp.bfloat16)


def smooth_x(scaled, before, after, tiles_x, labels, first, behind=()):
    slots, slab_x, wide = scaled.shape
    classes, tiles, rows, window = tiles_x.shape

    def body(mid_ref, before_ref, after_ref, tiles_ref, label_ref, *refs):
        out_ref, low_ref, high_ref, cat_ref = refs[len(behind) :]
        cat_ref[:BAND] = before_ref[0]
        cat_ref[BAND : BAND + slab_x] = mid_ref[0]
        cat_ref[BAND + slab_x :] = after_ref[0]
        label = label_ref[0]
        for t in range(tiles):
            columns = cat_ref[t * rows : t * rows + window]
            total = jnp.dot(tiles_ref[0, t], columns, preferred_element_type=jnp.float32)
            for level in range(1, classes):
                product = jnp.dot(tiles_ref[level, t], columns, preferred_element_type=jnp.float32)
                total = jnp.where(label == level, product, total)
            bounded = (soft_bound * jnp.tanh(total / soft_bound)).astype(jnp.bfloat16)
            out_ref[0, t * rows : (t + 1) * rows] = bounded
            low_ref[0, t * rows : (t + 1) * rows] = bounded[:, :BAND]
            high_ref[0, t * rows : (t + 1) * rows] = bounded[:, wide - BAND :]

    full = pl.BlockSpec((1, slab_x, wide), lambda m: (m, 0, 0))
    edge = pl.BlockSpec((1, BAND, wide), lambda m: (m, 0, 0))
    side = pl.BlockSpec((1, slab_x, BAND), lambda m: (m, 0, 0))
    size = slots * slab_x * wide
    return pl.pallas_call(
        body,
        grid=(slots,),
        in_specs=[
            full,
            edge,
            edge,
            pl.BlockSpec(tiles_x.shape, lambda m: (0, 0, 0, 0)),
            pl.BlockSpec((1, 1, wide), lambda m: (first + m, 0, 0)),
        ]
        + [pl.BlockSpec(memory_space=pl.ANY)] * len(behind),
        out_specs=[full, side, side],
        out_shape=[
            jax.ShapeDtypeStruct((slots, slab_x, wide), jnp.bfloat16),
            jax.ShapeDtypeStruct((slots, slab_x, BAND), jnp.bfloat16),
            jax.ShapeDtypeStruct((slots, slab_x, BAND), jnp.bfloat16),
        ],
        scratch_shapes=[pltpu.VMEM((slab_x + 2 * BAND, wide), jnp.bfloat16)],
        compiler_params=params(),
        cost_estimate=cost(2 * classes * window * size, 6 * size, size),
        name="smooth_x",
    )(scaled, before, after, tiles_x, labels, *behind)


def smooth_y(bounded, before, after, tiles_y, labels, place, first, behind=()):
    slots, slab_x, wide = bounded.shape
    classes, tiles, window, narrow = tiles_y.shape

    def body(place_ref, mid_ref, before_ref, after_ref, tiles_ref, label_ref, *refs):
        keep_ref, send_ref, cat_ref = refs[len(behind) :]
        cat_ref[:, :BAND] = before_ref[0]
        cat_ref[:, BAND : BAND + wide] = mid_ref[0]
        cat_ref[:, BAND + wide :] = after_ref[0]
        label = label_ref[0]
        left = place_ref[0] == 0
        halves = []
        for t in range(tiles):
            columns = cat_ref[:, t * narrow : t * narrow + window]
            total = jnp.dot(columns, tiles_ref[0, t], preferred_element_type=jnp.float32)
            for level in range(1, classes):
                product = jnp.dot(columns, tiles_ref[level, t], preferred_element_type=jnp.float32)
                total = jnp.where(label == level, product, total)
            halves.append(total.astype(jnp.bfloat16))
        keep_ref[0] = jnp.where(left, halves[0], halves[1])
        send_ref[0] = jnp.where(left, halves[1], halves[0])

    full = pl.BlockSpec((1, slab_x, wide), lambda m, place_ref: (m, 0, 0))
    side = pl.BlockSpec((1, slab_x, BAND), lambda m, place_ref: (m, 0, 0))
    block = pl.BlockSpec((1, slab_x, narrow), lambda m, place_ref: (m, 0, 0))
    size = slots * slab_x * wide
    out = jax.ShapeDtypeStruct((slots, slab_x, narrow), jnp.bfloat16)
    return pl.pallas_call(
        body,
        grid_spec=pltpu.PrefetchScalarGridSpec(
            num_scalar_prefetch=1,
            grid=(slots,),
            in_specs=[
                full,
                side,
                side,
                pl.BlockSpec(tiles_y.shape, lambda m, place_ref: (0, 0, 0, 0)),
                pl.BlockSpec((1, slab_x, 1), lambda m, place_ref: (first + m, 0, 0)),
            ]
            + [pl.BlockSpec(memory_space=pl.ANY)] * len(behind),
            out_specs=[block, block],
            scratch_shapes=[pltpu.VMEM((slab_x, wide + 2 * BAND), jnp.bfloat16)],
        ),
        out_shape=[out, out],
        compiler_params=params(),
        cost_estimate=cost(2 * classes * window * size, 6 * size),
        name="smooth_y",
    )(place, bounded, before, after, tiles_y, labels, *behind)


def join_planes(kept, came, perm_back, slots_of, planes, kernels, kernel_id, rows, base=()):
    _, slab_x, narrow = kept[0].shape
    span = perm_back.shape[0]
    sub = span // planes
    half = planes // PAIR
    count = len(kept)

    def body(*refs):
        kept_refs, came_refs = refs[:count], refs[count : 2 * count]
        perm_ref = refs[2 * count]
        out_ref, stack_ref = refs[-2:]
        for b in range(rows // sub):
            at = slice(b * sub, (b + 1) * sub)
            for j in range(half):
                c, m = slots_of[j]
                stack_ref[j * sub : (j + 1) * sub] = kept_refs[c][m, at]
                stack_ref[(half + j) * sub : (half + j + 1) * sub] = came_refs[c][m, at]
            moved = jnp.dot(perm_ref[...], stack_ref[...], preferred_element_type=jnp.float32)
            out_ref[at, 0] = moved.reshape(sub, planes, narrow).astype(jnp.bfloat16)

    specs = [pl.BlockSpec((a.shape[0], rows, narrow), lambda i: (0, i, 0)) for a in kept]
    size = slab_x * planes * narrow
    return pl.pallas_call(
        body,
        grid=(slab_x // rows,),
        in_specs=specs
        + specs
        + [pl.BlockSpec(perm_back.shape, lambda i: (0, 0))]
        + [pl.BlockSpec(memory_space=pl.ANY)] * len(base),
        out_specs=pl.BlockSpec((rows, 1, planes, narrow), lambda i: (i, kernel_id, 0, 0)),
        out_shape=jax.ShapeDtypeStruct((slab_x, kernels, planes, narrow), jnp.bfloat16),
        scratch_shapes=[pltpu.VMEM((span, narrow), jnp.bfloat16)],
        input_output_aliases={2 * count + 1: 0} if base else {},
        compiler_params=params(),
        cost_estimate=cost(2 * span * size, 4 * size),
        name="join_planes",
    )(*kept, *came, perm_back, *base)


def per_device(partial_kernels, illumination, classes_x, classes_y, widths_x, widths_y):
    _, slab_x, kernels, planes, full_y = partial_kernels.shape
    groups = lax.axis_size("ev")
    owners = lax.axis_size("gx")
    slab_y = full_y // groups
    full_x = slab_x * owners
    shards = groups // PAIR
    half = planes // PAIR
    me = lax.axis_index("ev")
    pair = lax.rem(me, PAIR)
    line = me // PAIR
    place = pair.astype(jnp.int32).reshape(1)

    other = [(i, i ^ 1) for i in range(groups)]
    z_up = [(i, i + PAIR) for i in range(groups - PAIR)]
    z_down = [(b, a) for a, b in z_up]
    x_up = [(i, i + 1) for i in range(owners - 1)]
    x_down = [(b, a) for a, b in x_up]
    lines = [[z * PAIR + y for z in range(shards)] for y in range(PAIR)]

    def over_line(parts):
        return lax.psum_scatter(
            parts, "ev", scatter_dimension=0, axis_index_groups=lines, tiled=True
        ).reshape(parts.shape[1:])

    sub = 256 // planes
    span = sub * planes
    to_row = lax.broadcasted_iota(jnp.int32, (span, span), 0)
    from_row = lax.broadcasted_iota(jnp.int32, (span, span), 1)
    plane_of = lax.rem(to_row // sub + half * pair, planes)
    perm = (from_row == lax.rem(to_row, sub) * planes + plane_of).astype(jnp.bfloat16)
    chunks = plan_chunks(kernels, half)

    lit_planes = jnp.transpose(illumination, (1, 0, 2))
    lit = lax.dynamic_slice_in_dim(lit_planes, half * pair, half, 0)
    lit_sent = lax.dynamic_slice_in_dim(lit_planes, half * (1 - pair), half, 0).astype(jnp.bfloat16)

    lit_pair = lax.ppermute(lit_sent, "ev", other)
    split, before = {}, []
    for some in (chunks[:1], chunks[1:2], chunks[2:]):
        for k in range(kernels):
            mine = [c for c in some if c[1] == k]
            if mine:
                arrays = list(split_planes(partial_kernels, perm, k, mine, shards, slab_x, before))
                before = arrays[:1]
                for c in mine:
                    split[c] = (arrays.pop(0),) if c[0] == "zy" else (arrays.pop(0), arrays.pop(0))

    labels_mine = lax.dynamic_slice_in_dim(classes_x, half * pair, half, 0)
    labels_sent = lax.dynamic_slice_in_dim(classes_x, half * (1 - pair), half, 0)
    labels_pair = lax.ppermute(labels_sent, "ev", other)
    labels_x = jnp.where(
        pair == 0,
        jnp.concatenate([labels_mine, labels_pair], 1),
        jnp.concatenate([labels_pair, labels_mine], 1),
    ).reshape(half, 1, PAIR * slab_y)
    labels_y = lax.dynamic_slice_in_dim(classes_y.T, half * pair, half, 0).reshape(half, slab_x, 1)

    tile = min(256, slab_x)
    tiles_x = band_tiles(full_x, widths_x, lax.axis_index("gx") * slab_x, slab_x // tile, tile)
    tiles_y = jnp.swapaxes(band_tiles(full_y, widths_y, line * PAIR * slab_y, PAIR, slab_y), 2, 3)

    slots_of, added, sums, kept, came = {}, {}, {}, {}, {}
    for n, (order, k, first, slots) in enumerate(chunks):
        for m in range(slots):
            slots_of[k * half + first + m] = (n, m)

    def begin(n, after=(), behind=()):
        order, k, first, slots = chunks[n]
        if order == "yz":
            own, sent = split[chunks[n]]
            if behind:
                sent = hold(sent, behind)
            added[n] = add_parts(own, lax.ppermute(sent, "ev", other), after)
            sums[n] = [over_line(added[n])]
        else:
            both = over_line(split[chunks[n]][0])
            sums[n] = [both[:slots], lax.ppermute(both[slots:], "ev", other)]

    scaled, sides = {}, {}

    def divide(n, after=()):
        order, k, first, slots = chunks[n]
        scaled[n], top, bottom = scale(sums[n], lit, lit_pair, place, first, after)
        sides[n] = lax.ppermute(bottom, "gx", x_up), lax.ppermute(top, "gx", x_down)

    bounded, ends = {}, {}

    def cross_x(n, after=()):
        order, k, first, slots = chunks[n]
        bounded[n], low, high = smooth_x(scaled[n], *sides[n], tiles_x, labels_x, first, after)
        ends[n] = lax.ppermute(high, "ev", z_up), lax.ppermute(low, "ev", z_down)

    def cross_y(n, after=()):
        order, k, first, slots = chunks[n]
        kept[n], send = smooth_y(bounded[n], *ends[n], tiles_y, labels_y, place, first, after)
        came[n] = lax.ppermute(send, "ev", other)

    last = len(chunks)
    begin(0)
    begin(1, [split[c][0] for c in chunks[2:]], [lit_pair, labels_pair])
    begin(2, [sums[0][0]])
    divide(1)
    cross_x(1)
    cross_y(1)
    begin(3, [kept[1], sums[0][1]])
    divide(0)
    cross_x(0)
    cross_y(0)
    for n in range(4, last):
        begin(n, [kept[0]])
    divide(2)
    divide(3, [came[1]])
    cross_x(2, [scaled[3]])
    cross_x(3)
    cross_y(2, [bounded[3]])
    cross_y(3)
    for n in range(4, last):
        divide(n, [kept[n - 1], came[0], came[2]])
        cross_x(n)
        cross_y(n)
    base = ()
    for k in range(kernels):
        mine = [n for n in range(last) if chunks[n][1] == k]
        where = [slots_of[k * half + j] for j in range(half)]
        where = [(mine.index(n), m) for n, m in where]
        parts = [kept[n] for n in mine], [came[n] for n in mine]
        base = (join_planes(*parts, perm.T, where, planes, kernels, k, slab_x // 2, base),)
    return base[0]


def solution(mesh):
    return jax.shard_map(
        per_device,
        mesh=mesh,
        in_specs=(
            P("ev", "gx", None, None, None),
            P("gx", None, "ev"),
            P(None, "ev"),
            P("gx", None),
            P(),
            P(),
        ),
        out_specs=P("gx", None, None, "ev"),
        check_vma=False,
    )
```
